128 devices in a mesh: tile: 8 (over y, x_hi), atom: 16 (over x_lo, z, core).
Axes of the slice: x: 4 (x_hi: 2, x_lo: 2; x = x_hi * 2 + x_lo), y: 4, z: 4, core: 2. Of those that a mesh axis runs over, the one named last changes fastest.
Arguments:
- image: bfloat16 [64, 64, 512], P(None, 'tile'), may hold values from -10 to 10
- coeffs: bfloat16 [512, 64, 512], P('atom', 'tile'), may hold values from -5 to 5
- dictionary: bfloat16 [512, 5184], P('atom'), may hold values from -0.078125 to 0.078125
- shrink: float32 [512], P('atom'), may hold values from 0.05 to 0.5
- seam_map: int32 [8, 512], replicated, may hold values from 0 to 1
Outputs:
- new_coeffs: bfloat16 [512, 64, 512], P('atom', 'tile')
- residual: bfloat16 [64, 64, 512], P(None, 'tile')
- atom_step: float32 [512, 5184], P('atom', 'tile')
The draws below stay inside these ranges and needn't reach their ends.
All inputs are finite; a program needn't handle non-finite values.
Results may differ from the reference program's by a relative error of at most 0.0029.
Values may be sent and summed in bfloat16 or wider, within the bound.
No kernel may reach another device: no remote copies, remote signals or barrier semaphores. Data moves between devices by JAX's collectives and lax.ppermute only.
A program may use at most 64 MiB of HBM per device.

```python
import math
import jax
import jax.numpy as jnp
from jax import lax

C = 64
K = 512
TAP = 9
TILE_W = 512
STRIPS = 8
H = 64


def plant(entries, rng, least, largest):
    extent = entries.shape
    index_at = [jax.random.randint(jax.random.fold_in(rng, axis), (), 0, extent[axis]) for axis in range(len(extent))]
    entries = entries.at[tuple(index_at)].set(least)
    longest = extent.index(max(extent))
    index_at[longest] = (index_at[longest] + 1) % extent[longest]
    return entries.at[tuple(index_at)].set(largest)


def shard_levels(key, dims, pieces, smallest, top_value):
    level = 1.0
    for axis_at, blocks in pieces:
        heights = jax.random.uniform(jax.random.fold_in(jax.random.fold_in(key, 6), axis_at), (blocks,), jnp.float32, smallest / len(pieces), top_value / len(pieces))
        level = level * jnp.repeat(jnp.exp(heights), dims[axis_at] // blocks).reshape((-1,) + (1,) * (len(dims) - 1 - axis_at))
    return level


def gaussian(own_key, dims, spread, bound, cuts=(), kind=jnp.bfloat16):
    drawn = spread * jax.random.normal(own_key, dims, jnp.float32)
    if cuts:
        drawn = drawn * shard_levels(own_key, dims, cuts, -0.22, 0.18)
    return jnp.clip(drawn, -bound, bound).astype(kind)


def setup_inputs(seed: int = 0) -> dict:
    streams_of = jax.random.split(jax.random.key(seed), 6)
    return {
        "image": gaussian(streams_of[0], (C, H, TILE_W), 2.0, 10.0, ((1, 8),)),
        "coeffs": gaussian(streams_of[1], (K, H, TILE_W), 1.0, 5.0, ((0, 16), (1, 8))),
        "dictionary": gaussian(streams_of[2], (K, C * TAP * TAP), (C * TAP * TAP) ** -0.5, 0.078125, ((0, 16),)),
        "shrink": jnp.clip(jnp.exp(math.log(0.5) - 2.3025851 * jax.random.uniform(streams_of[3], (K,), jnp.float32) ** shard_levels(streams_of[3], (K,), ((0, 16),), -0.2, 0.2)), 0.05, 0.5),
        "seam_map": plant(jax.random.randint(streams_of[4], (STRIPS, TILE_W), 0, 2), jax.random.fold_in(streams_of[4], 1), 0, 1).astype(jnp.int32),
    }


step_size = 0.1
eps_sq = 0.01

def pad_strips(field, seam_map):
    chans, rows, cols = field.shape
    strips = seam_map.shape[0]
    strip_rows = rows // strips
    tiled = field.reshape(chans, strips, strip_rows, cols).transpose(1, 0, 2, 3)
    w_down = (0.5 + 0.5 * seam_map.astype(jnp.float32)).astype(field.dtype)
    w_up = jnp.roll(w_down, 1, axis=0)
    upper = jnp.roll(tiled, 1, axis=0)[:, :, strip_rows - 4:] * w_up[:, None, None, :]
    lower = jnp.roll(tiled, -1, axis=0)[:, :, :4] * w_down[:, None, None, :]
    joined = jnp.concatenate([upper, tiled, lower], axis=2)
    return jnp.pad(joined, ((0, 0), (0, 0), (0, 0), (4, 4)))

def correlate(lhs, rhs):
    return lax.conv_general_dilated(lhs.astype(jnp.float32), rhs.astype(jnp.float32), (1, 1), 'VALID', dimension_numbers=('NCHW', 'OIHW', 'NCHW'), precision=lax.Precision.HIGHEST)

def reference(image, coeffs, dictionary, shrink, seam_map):
    strips = seam_map.shape[0]
    strip_rows = image.shape[1] // strips
    kernel = dictionary.reshape(K, C, TAP, TAP)
    coef_padded = pad_strips(coeffs, seam_map)
    synth_kernel = kernel.transpose(1, 0, 2, 3)

    def synth_one(block):
        return correlate(block[None], synth_kernel)[0]
    synthesis = lax.map(synth_one, coef_padded)
    image_tiles = image.reshape(C, strips, strip_rows, TILE_W).transpose(1, 0, 2, 3)
    resid_tiles = (image_tiles.astype(jnp.float32) - synthesis).astype(jnp.bfloat16)
    residual = resid_tiles.transpose(1, 0, 2, 3).reshape(C, H, TILE_W)
    resid_padded = pad_strips(residual, seam_map)
    coef_tiles = coeffs.reshape(K, strips, strip_rows, TILE_W).transpose(1, 0, 2, 3)
    flipped = kernel[:, :, ::-1, ::-1]

    def strip_terms(pair):
        padded, own = pair
        corr = correlate(padded[None], flipped)[0]
        terms = correlate(padded[:, None], own[:, None])
        return (corr, terms)
    corr_tiles, term_tiles = lax.map(strip_terms, (resid_padded, coef_tiles))
    correlation = corr_tiles.transpose(1, 0, 2, 3).reshape(K, H, TILE_W)
    updated = coeffs.astype(jnp.float32) + step_size * correlation
    new_coeffs = (updated - shrink[:, None, None] * updated / jnp.sqrt(updated * updated + eps_sq)).astype(jnp.bfloat16)
    summed = lax.optimization_barrier(jnp.sum(term_tiles, axis=0))
    scale = 1.0 / jnp.sqrt(jnp.float32(H * TILE_W))
    atom_step = summed[:, :, ::-1, ::-1].transpose(1, 0, 2, 3).reshape(K, C * TAP * TAP) * scale
    return (new_coeffs, residual, atom_step)
```

```python
import functools

import jax
import jax.numpy as jnp
from jax import lax
from jax.experimental import pallas as pl
from jax.experimental.pallas import tpu as pltpu
from jax.sharding import PartitionSpec as P

C = 64
TAP = 9
TILE_W = 512
HALO = TAP // 2
PADW = TILE_W + 256
LEFT = 128 - HALO

step_size = 0.1
eps_sq = 0.01


def rows_of(r, rows):
    return max(0, r - (TAP - 1)), min(rows - 1, r)


def shifted(row, j):
    n = row.shape[0]
    zero = jnp.zeros((n, 128), row.dtype)
    wide = jnp.concatenate([zero, row, zero], axis=1)
    return wide[:, LEFT + j : LEFT + j + TILE_W]


def synthesis_kernel(up_ref, own_ref, down_ref, wup_ref, wdown_ref, a_ref, out_ref, cols, acc):
    rows = own_ref.shape[0]
    atoms = own_ref.shape[1]
    acc[...] = jnp.zeros_like(acc)
    for r in range(rows + TAP - 1):
        if r < HALO:
            row = up_ref[r] * wup_ref[...]
        elif r < HALO + rows:
            row = own_ref[r - HALO]
        else:
            row = down_ref[r - HALO - rows] * wdown_ref[...]
        slot = r % 2
        for dx in range(TAP):
            cols[slot, dx * atoms : (dx + 1) * atoms, :] = shifted(row, dx)
        first, last = rows_of(r, rows)
        low, high = r - last, r - first
        part = jnp.dot(
            a_ref[low * C : (high + 1) * C, :], cols[slot], preferred_element_type=jnp.float32
        )
        base = (rows - 1 - last) * C
        acc[base : base + (high - low + 1) * C, :] += part
    for y in range(rows):
        out_ref[y] = acc[(rows - 1 - y) * C : (rows - y) * C, :].astype(out_ref.dtype)


def update_kernel(
    up_ref, own_ref, down_ref, wup_ref, wdown_ref, coef_ref, a_ref, shrink_ref,
    new_ref, term_ref, cols, acc, grad, scale,
):
    rows = own_ref.shape[0]
    atoms = coef_ref.shape[1]
    acc[...] = jnp.zeros_like(acc)
    grad[...] = jnp.zeros_like(grad)
    for r in range(rows + TAP - 1):
        if r < HALO:
            row = up_ref[r] * wup_ref[...]
        elif r < HALO + rows:
            row = own_ref[r - HALO]
        else:
            row = down_ref[r - HALO - rows] * wdown_ref[...]
        slot = r % 2
        for dx in range(TAP):
            cols[slot, dx * C : (dx + 1) * C, :] = shifted(row, TAP - 1 - dx)
        first, last = rows_of(r, rows)
        low, high = first + TAP - 1 - r, last + TAP - 1 - r
        acc[first * atoms : (last + 1) * atoms, :] += jnp.dot(
            a_ref[low * atoms : (high + 1) * atoms, :], cols[slot], preferred_element_type=jnp.float32
        )
        count = last - first + 1
        grad[low * atoms : (high + 1) * atoms, :] += lax.dot_general(
            coef_ref[first : last + 1].reshape(count * atoms, TILE_W),
            cols[slot],
            (((1,), (1,)), ((), ())),
            preferred_element_type=jnp.float32,
        )
    for y in range(rows):
        u = coef_ref[y].astype(jnp.float32) + step_size * acc[y * atoms : (y + 1) * atoms, :]
        new_ref[y] = (u - shrink_ref[...] * u / jnp.sqrt(u * u + eps_sq)).astype(new_ref.dtype)
    turned = jnp.transpose(grad[...]) * scale
    parts = term_ref.shape[0]
    per = C // parts
    for dx in range(TAP):
        for t in range(parts):
            term_ref[t, dx] = turned[dx * C + t * per : dx * C + (t + 1) * per, :]


def whole(count):
    return [pl.BlockSpec(memory_space=pltpu.VMEM)] * count


def per_device(image, coeffs, dictionary, shrink, seam_map):
    atoms = coeffs.shape[0]
    rows = image.shape[1]
    strips = lax.axis_size("tile")
    groups = lax.axis_size("atom")
    position = lax.axis_index("tile")
    member = lax.axis_index("atom") // 2
    seam_float = seam_map.astype(jnp.float32)
    w_down = (0.5 + 0.5 * seam_float[position]).astype(jnp.bfloat16)[None, :]
    w_up = (0.5 + 0.5 * seam_float[(position + strips - 1) % strips]).astype(jnp.bfloat16)[None, :]
    forward = [(i, (i + 1) % strips) for i in range(strips)]
    backward = [(i, (i + strips - 1) % strips) for i in range(strips)]
    chips = [[i for i in range(groups) if i % 2 == core] for core in range(2)]
    swap = [(i, i ^ 1) for i in range(groups)]

    def halos(field):
        up = lax.ppermute(field[rows - HALO :], "tile", forward)
        down = lax.ppermute(field[:HALO], "tile", backward)
        return up, down

    def exchange(field):
        return lax.all_to_all(field, "atom", 0, 0, tiled=True, axis_index_groups=chips)

    coef_rows = coeffs.transpose(1, 0, 2)
    kernel = dictionary.reshape(atoms, C, TAP, TAP)
    a_synth = kernel.transpose(2, 1, 3, 0).reshape(TAP * C, TAP * atoms)
    a_corr = kernel.transpose(2, 0, 3, 1).reshape(TAP * atoms, TAP * C)
    coef_up, coef_down = halos(coef_rows)
    params = pltpu.CompilerParams(vmem_limit_bytes=48 * 1024 * 1024)
    partial = pl.pallas_call(
        synthesis_kernel,
        out_shape=jax.ShapeDtypeStruct((rows, C, TILE_W), jnp.float32),
        in_specs=whole(6),
        out_specs=pl.BlockSpec(memory_space=pltpu.VMEM),
        scratch_shapes=[
            pltpu.VMEM((2, TAP * atoms, TILE_W), jnp.bfloat16),
            pltpu.VMEM((rows * C, TILE_W), jnp.float32),
        ],
        compiler_params=params,
    )(coef_up, coef_rows, coef_down, w_up, w_down, a_synth)
    pieces = exchange(partial.astype(jnp.float16))
    mine = jnp.sum(pieces.astype(jnp.float32), axis=0)
    mine = mine + lax.ppermute(mine, "atom", swap)
    image_row = lax.dynamic_index_in_dim(image, member, 1, keepdims=False)
    resid_row = (image_row.astype(jnp.float32) - mine).astype(jnp.bfloat16)
    resid_rows = exchange(jnp.broadcast_to(resid_row[None], (rows, C, TILE_W)))
    resid_up, resid_down = halos(resid_rows)
    residual = resid_rows.transpose(1, 0, 2)
    scale = float((rows * strips * TILE_W) ** -0.5)
    per = C // strips
    new_rows, terms = pl.pallas_call(
        functools.partial(update_kernel, scale=scale),
        out_shape=(
            jax.ShapeDtypeStruct((rows, atoms, TILE_W), jnp.bfloat16),
            jax.ShapeDtypeStruct((strips, TAP, per, TAP * atoms), jnp.float32),
        ),
        in_specs=whole(8),
        out_specs=(pl.BlockSpec(memory_space=pltpu.VMEM),) * 2,
        scratch_shapes=[
            pltpu.VMEM((2, TAP * C, TILE_W), jnp.bfloat16),
            pltpu.VMEM((rows * atoms, TILE_W), jnp.float32),
            pltpu.VMEM((TAP * atoms, TAP * C), jnp.float32),
        ],
        compiler_params=params,
    )(resid_up, resid_rows, resid_down, w_up, w_down, coef_rows, a_corr, shrink[:, None])
    new_coeffs = new_rows.transpose(1, 0, 2)
    got = lax.all_to_all(terms, "tile", 0, 0, tiled=True)
    step = jnp.sum(got, axis=0).reshape(TAP, per, TAP, atoms)
    atom_step = step.transpose(3, 1, 2, 0).reshape(atoms, per * TAP * TAP)
    return (new_coeffs, residual, atom_step)


def solution(mesh):
    placed = (P(None, "tile", None), P("atom", "tile", None), P("atom", None), P("atom"), P())
    return jax.shard_map(
        per_device,
        mesh=mesh,
        in_specs=placed,
        out_specs=(P("atom", "tile", None), P(None, "tile", None), P("atom", "tile")),
        check_vma=False,
    )
```

```python
import functools

import jax
import jax.numpy as jnp
from jax import lax
from jax.experimental import pallas as pl
from jax.experimental.pallas import tpu as pltpu
from jax.sharding import PartitionSpec as P

C = 64
TAP = 9
TAPS = TAP * TAP
TILE_W = 512
HALO = TAP // 2
LEFT = 128 - HALO
HALF = C // 2
ROWS = 8
TAP_ROWS = 88
LANES = 384
SHRINK_TERMS = 2.0**-5

step_size = 0.1
eps_sq = 0.01


def shifted(row, j):
    zero = jnp.zeros((row.shape[0], 128), row.dtype)
    wide = jnp.concatenate([zero, row, zero], axis=1)
    return wide[:, LEFT + j : LEFT + j + TILE_W]


def synthesis_kernel(
    core_ref, coef_ref, d_ref, wup_ref, wdown_ref,
    keep_ref, send_ref, acorr_ref,
    by_band, by_atom, turned, asynth, cols, acc,
):
    atoms = coef_ref.shape[1]
    d = d_ref[...].astype(jnp.float32)
    for c in range(C):
        by_band[c * atoms : (c + 1) * atoms, 0:TAPS] = d[:, c * TAPS : (c + 1) * TAPS]
    for k in range(atoms):
        block = by_band[pl.ds(k, C, stride=atoms), :]
        by_atom[k * TAP_ROWS : (k + 1) * TAP_ROWS, 0:C] = jnp.transpose(block)[0:TAP_ROWS, :]
    for tap in range(TAPS):
        dy, dx = divmod(tap, TAP)
        block = by_atom[pl.ds(tap, atoms, stride=TAP_ROWS), :][:, 0:C]
        acorr_ref[dy * atoms : (dy + 1) * atoms, dx * C : (dx + 1) * C] = block.astype(jnp.bfloat16)
        turned[dx * atoms : (dx + 1) * atoms, dy * C : (dy + 1) * C] = block
    asynth[...] = jnp.transpose(turned[...]).astype(jnp.bfloat16)

    acc[...] = jnp.zeros_like(acc)

    def add(slot, q, low, high):
        dy = low - (ROWS - 1) + q
        count = high - low + 1
        acc[low * C : (high + 1) * C, :] += jnp.dot(
            asynth[dy * C : (dy + count) * C, :], cols[slot], preferred_element_type=jnp.float32
        )

    for q in range(ROWS):
        row = coef_ref[q]
        weight = wup_ref[...] if q < HALO else wdown_ref[...]
        for slot, field in ((0, row), (1, row * weight)):
            for dx in range(TAP):
                cols[slot, dx * atoms : (dx + 1) * atoms, :] = shifted(field, dx)
        low, high = ROWS - 1 - q, ROWS + TAP - 2 - q
        add(0, q, max(HALO, low), min(HALO + ROWS - 1, high))
        if q < HALO:
            add(1, q, HALO + ROWS, high)
        else:
            add(1, q, low, HALO - 1)
    core = core_ref[0]
    mine = pl.multiple_of(core * HALF, HALF)
    other = pl.multiple_of((1 - core) * HALF, HALF)
    for j in range(ROWS):
        edge = HALO + ROWS + (HALO - 1) - j if j < HALO else ROWS - 1 - j
        for part, at in ((0, HALO + ROWS - 1 - j), (1, edge)):
            keep_ref[j, part] = acc[pl.ds(at * C + mine, HALF), :]
            send_ref[j, part] = acc[pl.ds(at * C + other, HALF), :].astype(send_ref.dtype)


def pad_row(core, mine_ref, other_ref, wup_ref, wdown_ref, r):
    if r < HALO:
        at, part = r, 1
    elif r < HALO + ROWS:
        at, part = r - HALO, 0
    else:
        at, part = r - ROWS, 1
    mine, other = mine_ref[at, part], other_ref[at, part]
    first = core == 0
    row = jnp.concatenate(
        [jnp.where(first, mine, other), jnp.where(first, other, mine)], axis=0
    )
    if r < HALO:
        return row * wup_ref[...]
    if r >= HALO + ROWS:
        return row * wdown_ref[...]
    return row


def met(r):
    first, last = max(0, r - (TAP - 1)), min(ROWS - 1, r)
    return first, last, first + TAP - 1 - r, last + TAP - 1 - r


def terms_kernel(
    core_ref, mine_ref, other_ref, wup_ref, wdown_ref, coef_ref, term_ref, cols, grad, scale
):
    atoms = coef_ref.shape[1]
    core = core_ref[0]
    grad[...] = jnp.zeros_like(grad)
    for r in range(ROWS + TAP - 1):
        row = pad_row(core, mine_ref, other_ref, wup_ref, wdown_ref, r)
        slot = r % 2
        for dx in range(TAP):
            cols[slot, dx * C : (dx + 1) * C, :] = shifted(row, TAP - 1 - dx)
        first, last, low, high = met(r)
        grad[low * atoms : (high + 1) * atoms, :] += lax.dot_general(
            coef_ref[first : last + 1].reshape((last - first + 1) * atoms, TILE_W),
            cols[slot],
            (((1,), (1,)), ((), ())),
            preferred_element_type=jnp.float32,
        )
    turned = jnp.transpose(grad[...]) * scale
    parts = term_ref.shape[0]
    per = C // parts
    term_ref[...] = jnp.zeros_like(term_ref)
    for dx in range(TAP):
        for t in range(parts):
            term_ref[t, dx * per : (dx + 1) * per, 0 : TAP * atoms] = turned[
                dx * C + t * per : dx * C + (t + 1) * per, :
            ].astype(term_ref.dtype)


def coeffs_kernel(
    core_ref, mine_ref, other_ref, wup_ref, wdown_ref, coef_ref, a_ref, shrink_ref,
    new_ref, cols, acc,
):
    atoms = coef_ref.shape[1]
    core = core_ref[0]
    acc[...] = jnp.zeros_like(acc)
    for r in range(ROWS + TAP - 1):
        row = pad_row(core, mine_ref, other_ref, wup_ref, wdown_ref, r)
        slot = r % 2
        for dx in range(TAP):
            cols[slot, dx * C : (dx + 1) * C, :] = shifted(row, TAP - 1 - dx)
        first, last, low, high = met(r)
        acc[first * atoms : (last + 1) * atoms, :] += jnp.dot(
            a_ref[low * atoms : (high + 1) * atoms, :], cols[slot], preferred_element_type=jnp.float32
        )
    for y in range(ROWS):
        u = coef_ref[y].astype(jnp.float32) + step_size * acc[y * atoms : (y + 1) * atoms, :]
        new_ref[y] = (u - shrink_ref[...] * u / jnp.sqrt(u * u + eps_sq)).astype(new_ref.dtype)


VMEM = pl.BlockSpec(memory_space=pltpu.VMEM)
SMEM = pl.BlockSpec(memory_space=pltpu.SMEM)


def per_device(image, coeffs, dictionary, shrink, seam_map):
    atoms = coeffs.shape[0]
    strips = lax.axis_size("tile")
    groups = lax.axis_size("atom")
    position = lax.axis_index("tile")
    atom_at = lax.axis_index("atom")
    member = atom_at // 2
    core = atom_at % 2
    core_at = core.astype(jnp.int32)[None]
    seam_float = seam_map.astype(jnp.float32)
    w_down = (0.5 + 0.5 * seam_float[position]).astype(jnp.bfloat16)[None, :]
    w_up = (0.5 + 0.5 * seam_float[(position + strips - 1) % strips]).astype(jnp.bfloat16)[None, :]
    chips = [[i for i in range(groups) if i % 2 == side] for side in range(2)]
    swap = [(i, i ^ 1) for i in range(groups)]
    half = groups // 2
    pairs = []
    for s in range(strips):
        for a in range(groups):
            if a < half:
                pairs.append((s * groups + a, (s + strips - 1) % strips * groups + a + half))
            else:
                pairs.append((s * groups + a, (s + 1) % strips * groups + a - half))

    def exchange(field):
        return lax.all_to_all(field, "atom", 0, 0, tiled=True, axis_index_groups=chips)

    coef_rows = coeffs.transpose(1, 0, 2)
    params = pltpu.CompilerParams(vmem_limit_bytes=48 * 1024 * 1024)
    flops = 2 * 72 * atoms * C * TAP * TILE_W
    cost = pl.CostEstimate(flops=flops, bytes_accessed=3 << 20, transcendentals=0)
    keep, send, a_corr = pl.pallas_call(
        synthesis_kernel,
        out_shape=(
            jax.ShapeDtypeStruct((ROWS, 2, HALF, TILE_W), jnp.float32),
            jax.ShapeDtypeStruct((ROWS, 2, HALF, TILE_W), jnp.float32),
            jax.ShapeDtypeStruct((TAP * atoms, TAP * C), jnp.bfloat16),
        ),
        in_specs=[SMEM] + [VMEM] * 4,
        out_specs=(VMEM,) * 3,
        scratch_shapes=[
            pltpu.VMEM((C * atoms, 128), jnp.float32),
            pltpu.VMEM((atoms * TAP_ROWS, 128), jnp.float32),
            pltpu.VMEM((TAP * atoms, TAP * C), jnp.float32),
            pltpu.VMEM((TAP * C, TAP * atoms), jnp.bfloat16),
            pltpu.VMEM((2, TAP * atoms, TILE_W), jnp.bfloat16),
            pltpu.VMEM((2 * ROWS * C, TILE_W), jnp.float32),
        ],
        compiler_params=params,
        cost_estimate=cost,
    )(core_at, coef_rows, dictionary, w_up, w_down)
    other = lax.ppermute(send.astype(jnp.float16), "atom", swap)
    pieces = exchange((keep + other.astype(jnp.float32)).astype(jnp.float16))
    total = jnp.sum(pieces.astype(jnp.float32), axis=0)
    image_row = lax.dynamic_slice(image, (core * HALF, member, 0), (HALF, 1, TILE_W))[:, 0]
    held = jnp.stack([image_row.astype(jnp.float32) - total[0], total[1]])
    facing = lax.ppermute(held, ("tile", "atom"), pairs)
    rows_two = jnp.stack([held[0] - facing[1], facing[0] - held[1]]).astype(jnp.bfloat16)
    mine = exchange(jnp.broadcast_to(rows_two[None], (ROWS, 2, HALF, TILE_W)))
    theirs = lax.ppermute(mine, "atom", swap)

    scale = float((ROWS * strips * TILE_W) ** -0.5) * SHRINK_TERMS
    per = C // strips
    terms = pl.pallas_call(
        functools.partial(terms_kernel, scale=scale),
        out_shape=jax.ShapeDtypeStruct((strips, TAP * per, LANES), jnp.float32),
        in_specs=[SMEM] + [VMEM] * 5,
        out_specs=VMEM,
        scratch_shapes=[
            pltpu.VMEM((2, TAP * C, TILE_W), jnp.bfloat16),
            pltpu.VMEM((TAP * atoms, TAP * C), jnp.float32),
        ],
        compiler_params=params,
        cost_estimate=cost,
    )(core_at, mine, theirs, w_up, w_down, coef_rows)
    got = lax.all_to_all(terms.astype(jnp.float16), "tile", 0, 0, tiled=True)
    new_rows = pl.pallas_call(
        coeffs_kernel,
        out_shape=jax.ShapeDtypeStruct((ROWS, atoms, TILE_W), jnp.bfloat16),
        in_specs=[SMEM] + [VMEM] * 7,
        out_specs=VMEM,
        scratch_shapes=[
            pltpu.VMEM((2, TAP * C, TILE_W), jnp.bfloat16),
            pltpu.VMEM((ROWS * atoms, TILE_W), jnp.float32),
        ],
        compiler_params=params,
        cost_estimate=cost,
    )(core_at, mine, theirs, w_up, w_down, coef_rows, a_corr, shrink[:, None])
    new_coeffs = new_rows.transpose(1, 0, 2)
    own_half, other_half = mine[:, 0], theirs[:, 0]
    residual = jnp.concatenate(
        [
            jnp.where(core == 0, own_half, other_half),
            jnp.where(core == 0, other_half, own_half),
        ],
        axis=1,
    ).transpose(1, 0, 2)
    step = jnp.sum(got.astype(jnp.float32), axis=0)[:, : TAP * atoms] * (1.0 / SHRINK_TERMS)
    step = step.reshape(TAP, per, TAP, atoms)
    atom_step = step.transpose(3, 1, 2, 0).reshape(atoms, per * TAPS)
    return (new_coeffs, residual, atom_step)


def solution(mesh):
    placed = (P(None, "tile", None), P("atom", "tile", None), P("atom", None), P("atom"), P())
    return jax.shard_map(
        per_device,
        mesh=mesh,
        in_specs=placed,
        out_specs=(P("atom", "tile", None), P(None, "tile", None), P("atom", "tile")),
        check_vma=False,
    )
```

```python
import functools

import jax
import jax.numpy as jnp
from jax import lax
from jax.experimental import pallas as pl
from jax.experimental.pallas import tpu as pltpu
from jax.sharding import PartitionSpec as P

C = 64
TAP = 9
TAPS = TAP * TAP
TILE_W = 512
HALO = TAP // 2
LEFT = 128 - HALO
HALF = C // 2
ROWS = 8
TAP_ROWS = 88
LANES = 384
SHRINK_TERMS = 2.0**-5

step_size = 0.1
eps_sq = 0.01


def seam_weight(seam_ref, at):
    seam = seam_ref[pl.ds(at, 1), :].astype(jnp.float32)
    return (0.5 + 0.5 * seam).astype(jnp.bfloat16)


def turn(block):
    return jnp.swapaxes(block.astype(jnp.float32), 0, 1).astype(jnp.bfloat16)


def shifted(row, j):
    zero = jnp.zeros((row.shape[0], 128), row.dtype)
    wide = jnp.concatenate([zero, row, zero], axis=1)
    return wide[:, LEFT + j : LEFT + j + TILE_W]


def synthesis_kernel(
    coef_hbm, d_hbm, seam_hbm,
    keep_ref, send_ref, acorr_ref, rows_ref, edge_ref,
    coef_ref, d_ref, seam_ref, by_band, by_atom, turned, asynth, cols, acc, sems,
):
    atoms = coef_ref.shape[0]
    copies = [
        pltpu.make_async_copy(source, target, sems.at[i])
        for i, (source, target) in enumerate(
            ((d_hbm, d_ref), (coef_hbm, coef_ref), (seam_hbm, seam_ref))
        )
    ]
    for copy in copies:
        copy.start()
    copies[0].wait()
    d = d_ref[...].astype(jnp.float32)
    for c in range(C):
        by_band[c * atoms : (c + 1) * atoms, 0:TAPS] = d[:, c * TAPS : (c + 1) * TAPS]
    for k in range(atoms):
        block = by_band[pl.ds(k, C, stride=atoms), :]
        by_atom[k * TAP_ROWS : (k + 1) * TAP_ROWS, 0:C] = jnp.transpose(block)[0:TAP_ROWS, :]
    for tap in range(TAPS):
        dy, dx = divmod(tap, TAP)
        block = by_atom[pl.ds(tap, atoms, stride=TAP_ROWS), :][:, 0:C]
        acorr_ref[dy * atoms : (dy + 1) * atoms, dx * C : (dx + 1) * C] = block.astype(jnp.bfloat16)
        turned[dx * atoms : (dx + 1) * atoms, dy * C : (dy + 1) * C] = block
    asynth[...] = jnp.transpose(turned[...]).astype(jnp.bfloat16)

    copies[1].wait()
    copies[2].wait()
    position = lax.axis_index("tile")
    strips = seam_ref.shape[0]
    w_up = seam_weight(seam_ref, lax.rem(position + (strips - 1), strips))
    w_down = seam_weight(seam_ref, position)
    edge_ref[0:1, :] = w_up
    edge_ref[1:2, :] = w_down
    rows_ref[...] = turn(coef_ref[...])
    acc[...] = jnp.zeros_like(acc)

    def add(slot, q, low, high):
        dy = low - (ROWS - 1) + q
        count = high - low + 1
        acc[low * C : (high + 1) * C, :] += jnp.dot(
            asynth[dy * C : (dy + count) * C, :], cols[slot], preferred_element_type=jnp.float32
        )

    for q in range(ROWS):
        row = rows_ref[q]
        weight = w_up if q < HALO else w_down
        for slot, field in ((0, row), (1, row * weight)):
            for dx in range(TAP):
                cols[slot, dx * atoms : (dx + 1) * atoms, :] = shifted(field, dx)
        low, high = ROWS - 1 - q, ROWS + TAP - 2 - q
        add(0, q, max(HALO, low), min(HALO + ROWS - 1, high))
        if q < HALO:
            add(1, q, HALO + ROWS, high)
        else:
            add(1, q, low, HALO - 1)
    core = lax.rem(lax.axis_index("atom"), 2)
    mine = pl.multiple_of(core * HALF, HALF)
    other = pl.multiple_of((1 - core) * HALF, HALF)
    for j in range(ROWS):
        edge = HALO + ROWS + (HALO - 1) - j if j < HALO else ROWS - 1 - j
        for part, at in ((0, HALO + ROWS - 1 - j), (1, edge)):
            keep_ref[j, part] = acc[pl.ds(at * C + mine, HALF), :]
            send_ref[j, part] = acc[pl.ds(at * C + other, HALF), :].astype(send_ref.dtype)


def pad_row(core, mine_ref, other_ref, w_up, w_down, r):
    if r < HALO:
        at, part = r, 1
    elif r < HALO + ROWS:
        at, part = r - HALO, 0
    else:
        at, part = r - ROWS, 1
    mine, other = mine_ref[at, part], other_ref[at, part]
    first = core == 0
    row = jnp.concatenate(
        [jnp.where(first, mine, other), jnp.where(first, other, mine)], axis=0
    )
    if r < HALO:
        return row * w_up
    if r >= HALO + ROWS:
        return row * w_down
    return row


def met(r):
    first, last = max(0, r - (TAP - 1)), min(ROWS - 1, r)
    return first, last, first + TAP - 1 - r, last + TAP - 1 - r


def terms_kernel(half_ref, edge_ref, coef_ref, term_ref, cols, lags, scale):
    atoms = coef_ref.shape[1]
    wide = ROWS * TILE_W
    sums = []
    for part in range(2):
        for i in range(ROWS):
            r = part * ROWS + i
            if r < HALO:
                row = half_ref[r, 1] * edge_ref[0:1, :]
            elif r < HALO + ROWS:
                row = half_ref[r - HALO, 0]
            else:
                row = half_ref[r - ROWS, 1] * edge_ref[1:2, :]
            columns = slice(i * TILE_W, (i + 1) * TILE_W)
            for dx in range(TAP):
                cols[part, dx * HALF : (dx + 1) * HALF, columns] = shifted(row, TAP - 1 - dx)
            for at in range(ROWS):
                y = r - (ROWS - 1) - part + at
                there = 0 <= y < ROWS
                lags[part, at * atoms : (at + 1) * atoms, columns] = (
                    coef_ref[y] if there else jnp.zeros((atoms, TILE_W), jnp.bfloat16)
                )
        sums.append(
            lax.dot_general(
                cols[part], lags[part], (((1,), (1,)), ((), ())), preferred_element_type=jnp.float32
            )
        )
    edge = jnp.zeros((TAP * HALF, atoms), jnp.float32)
    total = jnp.concatenate([edge, sums[0]], axis=1) + jnp.concatenate([sums[1], edge], axis=1)
    total = jnp.concatenate(
        [total * scale, jnp.zeros((TAP * HALF, LANES - TAP * atoms), jnp.float32)], axis=1
    )
    parts = term_ref.shape[0]
    per = HALF // parts
    for dx in range(TAP):
        for t in range(parts):
            term_ref[t, dx * per : (dx + 1) * per, :] = total[
                dx * HALF + t * per : dx * HALF + (t + 1) * per, :
            ]


def coeffs_kernel(
    mine_ref, other_ref, edge_ref, coef_ref, a_ref, shrink_ref,
    new_ref, resid_ref, cols, acc, own,
):
    atoms = coef_ref.shape[1]
    core = lax.rem(lax.axis_index("atom"), 2)
    w_up, w_down = edge_ref[0:1, :], edge_ref[1:2, :]
    acc[...] = jnp.zeros_like(acc)
    for r in range(ROWS + TAP - 1):
        row = pad_row(core, mine_ref, other_ref, w_up, w_down, r)
        if HALO <= r < HALO + ROWS:
            own[r - HALO] = row
        slot = r % 2
        for dx in range(TAP):
            cols[slot, dx * C : (dx + 1) * C, :] = shifted(row, TAP - 1 - dx)
        first, last, low, high = met(r)
        acc[first * atoms : (last + 1) * atoms, :] += jnp.dot(
            a_ref[low * atoms : (high + 1) * atoms, :], cols[slot], preferred_element_type=jnp.float32
        )
    u = coef_ref[...].reshape(ROWS * atoms, TILE_W).astype(jnp.float32) + step_size * acc[...]
    threshold = jnp.concatenate([shrink_ref[...]] * ROWS, axis=0)
    u = u - threshold * u / jnp.sqrt(u * u + eps_sq)
    new_ref[...] = turn(u.reshape(ROWS, atoms, TILE_W))
    resid_ref[...] = turn(own[...])


VMEM = pl.BlockSpec(memory_space=pltpu.VMEM)
HBM = pl.BlockSpec(memory_space=pltpu.HBM)


def per_device(image, coeffs, dictionary, shrink, seam_map):
    atoms = coeffs.shape[0]
    strips = lax.axis_size("tile")
    groups = lax.axis_size("atom")
    atom_at = lax.axis_index("atom")
    member = atom_at // 2
    core = atom_at % 2
    chips = [[i for i in range(groups) if i % 2 == side] for side in range(2)]
    swap = [(i, i ^ 1) for i in range(groups)]
    half = groups // 2
    pairs = []
    for s in range(strips):
        for a in range(groups):
            if a < half:
                pairs.append((s * groups + a, (s + strips - 1) % strips * groups + a + half))
            else:
                pairs.append((s * groups + a, (s + 1) % strips * groups + a - half))

    def exchange(field):
        return lax.all_to_all(field, "atom", 0, 0, tiled=True, axis_index_groups=chips)

    params = pltpu.CompilerParams(vmem_limit_bytes=48 * 1024 * 1024)
    flops = 2 * 72 * atoms * C * TAP * TILE_W
    cost = pl.CostEstimate(flops=flops, bytes_accessed=3 << 20, transcendentals=0)
    keep, send, a_corr, coef_rows, edges = pl.pallas_call(
        synthesis_kernel,
        out_shape=(
            jax.ShapeDtypeStruct((ROWS, 2, HALF, TILE_W), jnp.float32),
            jax.ShapeDtypeStruct((ROWS, 2, HALF, TILE_W), jnp.float32),
            jax.ShapeDtypeStruct((TAP * atoms, TAP * C), jnp.bfloat16),
            jax.ShapeDtypeStruct((ROWS, atoms, TILE_W), jnp.bfloat16),
            jax.ShapeDtypeStruct((2, TILE_W), jnp.bfloat16),
        ),
        in_specs=[HBM] * 3,
        out_specs=(VMEM,) * 5,
        scratch_shapes=[
            pltpu.VMEM(coeffs.shape, jnp.bfloat16),
            pltpu.VMEM(dictionary.shape, jnp.bfloat16),
            pltpu.VMEM(seam_map.shape, jnp.int32),
            pltpu.VMEM((C * atoms, 128), jnp.float32),
            pltpu.VMEM((atoms * TAP_ROWS, 128), jnp.float32),
            pltpu.VMEM((TAP * atoms, TAP * C), jnp.float32),
            pltpu.VMEM((TAP * C, TAP * atoms), jnp.bfloat16),
            pltpu.VMEM((2, TAP * atoms, TILE_W), jnp.bfloat16),
            pltpu.VMEM((2 * ROWS * C, TILE_W), jnp.float32),
            pltpu.SemaphoreType.DMA((3,)),
        ],
        compiler_params=params,
        cost_estimate=cost,
    )(coeffs, dictionary, seam_map)
    image_row = lax.dynamic_slice(image, (core * HALF, member, 0), (HALF, 1, TILE_W))[:, 0]
    other = lax.ppermute(send.astype(jnp.float16), "atom", swap)
    partial = (keep + other.astype(jnp.float32)).astype(jnp.float16)
    partial, image_row, threshold = lax.optimization_barrier((partial, image_row, shrink[:, None]))
    pieces = exchange(partial)
    total = jnp.sum(pieces.astype(jnp.float32), axis=0)
    held = jnp.stack([image_row.astype(jnp.float32) - total[0], total[1]])
    facing = lax.ppermute(held, ("tile", "atom"), pairs)
    rows_two = jnp.stack([held[0] - facing[1], facing[0] - held[1]]).astype(jnp.bfloat16)
    mine = exchange(jnp.broadcast_to(rows_two[None], (ROWS, 2, HALF, TILE_W)))
    theirs = lax.ppermute(mine, "atom", swap)

    scale = float((ROWS * strips * TILE_W) ** -0.5) * SHRINK_TERMS
    per = C // strips
    term_half = pl.pallas_call(
        functools.partial(terms_kernel, scale=scale),
        out_shape=jax.ShapeDtypeStruct((strips // 2, TAP * per, LANES), jnp.float32),
        in_specs=[VMEM] * 3,
        out_specs=VMEM,
        scratch_shapes=[
            pltpu.VMEM((2, TAP * HALF, ROWS * TILE_W), jnp.bfloat16),
            pltpu.VMEM((2, ROWS * atoms, ROWS * TILE_W), jnp.bfloat16),
        ],
        compiler_params=params,
        cost_estimate=pl.CostEstimate(flops=flops // 2, bytes_accessed=3 << 20, transcendentals=0),
    )
    my_terms = term_half(mine, edges, coef_rows)
    their_terms = term_half(theirs, edges, coef_rows)
    first = core == 0
    terms = jnp.concatenate(
        [jnp.where(first, my_terms, their_terms), jnp.where(first, their_terms, my_terms)]
    ).astype(jnp.float16)
    got = lax.all_to_all(terms, "tile", 0, 0, tiled=True)
    new_coeffs, residual = pl.pallas_call(
        coeffs_kernel,
        out_shape=(
            jax.ShapeDtypeStruct((atoms, ROWS, TILE_W), jnp.bfloat16),
            jax.ShapeDtypeStruct((C, ROWS, TILE_W), jnp.bfloat16),
        ),
        in_specs=[VMEM] * 6,
        out_specs=(VMEM,) * 2,
        scratch_shapes=[
            pltpu.VMEM((2, TAP * C, TILE_W), jnp.bfloat16),
            pltpu.VMEM((ROWS * atoms, TILE_W), jnp.float32),
            pltpu.VMEM((ROWS, C, TILE_W), jnp.bfloat16),
        ],
        compiler_params=params,
        cost_estimate=cost,
    )(mine, theirs, edges, coef_rows, a_corr, threshold)
    step = jnp.sum(got.astype(jnp.float32), axis=0)[:, : TAP * atoms] * (1.0 / SHRINK_TERMS)
    step = step.reshape(TAP, per, TAP, atoms)
    atom_step = step.transpose(3, 1, 2, 0).reshape(atoms, per * TAPS)
    return (new_coeffs, residual, atom_step)


def solution(mesh):
    placed = (P(None, "tile", None), P("atom", "tile", None), P("atom", None), P("atom"), P())
    return jax.shard_map(
        per_device,
        mesh=mesh,
        in_specs=placed,
        out_specs=(P("atom", "tile", None), P(None, "tile", None), P("atom", "tile")),
        check_vma=False,
    )
```

```python
import functools

import jax
import jax.numpy as jnp
from jax import lax
from jax.experimental import pallas as pl
from jax.experimental.pallas import tpu as pltpu
from jax.sharding import PartitionSpec as P

C = 64
TAP = 9
TAPS = TAP * TAP
TILE_W = 512
HALO = TAP // 2
LEFT = 128 - HALO
HALF = C // 2
ROWS = 8
TAP_ROWS = 88
LANES = 384
SHRINK_TERMS = 2.0**-5

step_size = 0.1
eps_sq = 0.01


def seam_weight(seam_ref, at):
    seam = seam_ref[pl.ds(at, 1), :].astype(jnp.float32)
    return (0.5 + 0.5 * seam).astype(jnp.bfloat16)


def turn(block):
    return jnp.swapaxes(block.astype(jnp.float32), 0, 1).astype(jnp.bfloat16)


def shifted(row, j):
    zero = jnp.zeros((row.shape[0], 128), row.dtype)
    wide = jnp.concatenate([zero, row, zero], axis=1)
    return wide[:, LEFT + j : LEFT + j + TILE_W]


def atoms_kernel(d_ref, acorr_ref, asynth_ref, by_band, by_atom, turned):
    atoms = d_ref.shape[0]
    d = d_ref[...].astype(jnp.float32)
    for c in range(C):
        by_band[c * atoms : (c + 1) * atoms, 0:TAPS] = d[:, c * TAPS : (c + 1) * TAPS]
    for k in range(atoms):
        block = by_band[pl.ds(k, C, stride=atoms), :]
        by_atom[k * TAP_ROWS : (k + 1) * TAP_ROWS, 0:C] = jnp.transpose(block)[0:TAP_ROWS, :]
    for tap in range(TAPS):
        dy, dx = divmod(tap, TAP)
        block = by_atom[pl.ds(tap, atoms, stride=TAP_ROWS), :][:, 0:C]
        acorr_ref[dy * atoms : (dy + 1) * atoms, dx * C : (dx + 1) * C] = block.astype(jnp.bfloat16)
        turned[dx * atoms : (dx + 1) * atoms, dy * C : (dy + 1) * C] = block
    bands = jnp.transpose(turned[...]).astype(jnp.bfloat16)
    for dy in range(TAP):
        for half in range(2):
            asynth_ref[half, dy * HALF : (dy + 1) * HALF, :] = bands[
                dy * C + half * HALF : dy * C + (half + 1) * HALF, :
            ]


def synthesize(a, rows_ref, w_up, w_down, out_ref, cols, acc):
    atoms = rows_ref.shape[1]
    acc[...] = jnp.zeros_like(acc)

    def add(slot, q, low, high):
        dy = low - (ROWS - 1) + q
        count = high - low + 1
        acc[low * HALF : (high + 1) * HALF, :] += jnp.dot(
            a[dy * HALF : (dy + count) * HALF, :], cols[slot], preferred_element_type=jnp.float32
        )

    for q in range(ROWS):
        row = rows_ref[q]
        weight = w_up if q < HALO else w_down
        for slot, field in ((0, row), (1, row * weight)):
            for dx in range(TAP):
                cols[slot, dx * atoms : (dx + 1) * atoms, :] = shifted(field, dx)
        low, high = ROWS - 1 - q, ROWS + TAP - 2 - q
        add(0, q, max(HALO, low), min(HALO + ROWS - 1, high))
        if q < HALO:
            add(1, q, HALO + ROWS, high)
        else:
            add(1, q, low, HALO - 1)
    for j in range(ROWS):
        edge = HALO + ROWS + (HALO - 1) - j if j < HALO else ROWS - 1 - j
        for part, at in ((0, HALO + ROWS - 1 - j), (1, edge)):
            out_ref[j, part] = acc[at * HALF : (at + 1) * HALF, :]


def send_kernel(coef_ref, a_ref, seam_ref, send_ref, rows_ref, edge_ref, cols, acc):
    position = lax.axis_index("tile")
    strips = seam_ref.shape[0]
    w_up = seam_weight(seam_ref, lax.rem(position + (strips - 1), strips))
    w_down = seam_weight(seam_ref, position)
    edge_ref[0:1, :] = w_up
    edge_ref[1:2, :] = w_down
    rows_ref[...] = turn(coef_ref[...])
    a = a_ref[1 - lax.rem(lax.axis_index("atom"), 2)]
    synthesize(a, rows_ref, w_up, w_down, send_ref, cols, acc)


def keep_kernel(rows_ref, a_ref, edge_ref, keep_ref, cols, acc):
    a = a_ref[lax.rem(lax.axis_index("atom"), 2)]
    synthesize(a, rows_ref, edge_ref[0:1, :], edge_ref[1:2, :], keep_ref, cols, acc)


def pad_row(core, mine_ref, other_ref, w_up, w_down, r):
    if r < HALO:
        at, part = r, 1
    elif r < HALO + ROWS:
        at, part = r - HALO, 0
    else:
        at, part = r - ROWS, 1
    mine, other = mine_ref[at, part], other_ref[at, part]
    first = core == 0
    row = jnp.concatenate(
        [jnp.where(first, mine, other), jnp.where(first, other, mine)], axis=0
    )
    if r < HALO:
        return row * w_up
    if r >= HALO + ROWS:
        return row * w_down
    return row


def met(r):
    first, last = max(0, r - (TAP - 1)), min(ROWS - 1, r)
    return first, last, first + TAP - 1 - r, last + TAP - 1 - r


def terms_kernel(half_ref, edge_ref, coef_ref, term_ref, cols, lags, scale):
    atoms = coef_ref.shape[1]
    wide = ROWS * TILE_W
    sums = []
    for part in range(2):
        for i in range(ROWS):
            r = part * ROWS + i
            if r < HALO:
                row = half_ref[r, 1] * edge_ref[0:1, :]
            elif r < HALO + ROWS:
                row = half_ref[r - HALO, 0]
            else:
                row = half_ref[r - ROWS, 1] * edge_ref[1:2, :]
            columns = slice(i * TILE_W, (i + 1) * TILE_W)
            for dx in range(TAP):
                cols[part, dx * HALF : (dx + 1) * HALF, columns] = shifted(row, TAP - 1 - dx)
            for at in range(ROWS):
                y = r - (ROWS - 1) - part + at
                there = 0 <= y < ROWS
                lags[part, at * atoms : (at + 1) * atoms, columns] = (
                    coef_ref[y] if there else jnp.zeros((atoms, TILE_W), jnp.bfloat16)
                )
        sums.append(
            lax.dot_general(
                cols[part], lags[part], (((1,), (1,)), ((), ())), preferred_element_type=jnp.float32
            )
        )
    edge = jnp.zeros((TAP * HALF, atoms), jnp.float32)
    total = jnp.concatenate([edge, sums[0]], axis=1) + jnp.concatenate([sums[1], edge], axis=1)
    total = jnp.concatenate(
        [total * scale, jnp.zeros((TAP * HALF, LANES - TAP * atoms), jnp.float32)], axis=1
    )
    parts = term_ref.shape[0]
    per = HALF // parts
    for dx in range(TAP):
        for t in range(parts):
            term_ref[t, dx * per : (dx + 1) * per, :] = total[
                dx * HALF + t * per : dx * HALF + (t + 1) * per, :
            ]


def coeffs_kernel(
    mine_ref, other_ref, edge_ref, coef_ref, a_ref, shrink_ref,
    new_ref, resid_ref, cols, acc, own,
):
    atoms = coef_ref.shape[1]
    core = lax.rem(lax.axis_index("atom"), 2)
    w_up, w_down = edge_ref[0:1, :], edge_ref[1:2, :]
    acc[...] = jnp.zeros_like(acc)
    for r in range(ROWS + TAP - 1):
        row = pad_row(core, mine_ref, other_ref, w_up, w_down, r)
        if HALO <= r < HALO + ROWS:
            own[r - HALO] = row
        slot = r % 2
        for dx in range(TAP):
            cols[slot, dx * C : (dx + 1) * C, :] = shifted(row, TAP - 1 - dx)
        first, last, low, high = met(r)
        acc[first * atoms : (last + 1) * atoms, :] += jnp.dot(
            a_ref[low * atoms : (high + 1) * atoms, :], cols[slot], preferred_element_type=jnp.float32
        )
    u = coef_ref[...].reshape(ROWS * atoms, TILE_W).astype(jnp.float32) + step_size * acc[...]
    threshold = jnp.concatenate([shrink_ref[...]] * ROWS, axis=0)
    u = u - threshold * u / jnp.sqrt(u * u + eps_sq)
    new_ref[...] = turn(u.reshape(ROWS, atoms, TILE_W))
    resid_ref[...] = turn(own[...])


VMEM = pl.BlockSpec(memory_space=pltpu.VMEM)


def per_device(image, coeffs, dictionary, shrink, seam_map):
    atoms = coeffs.shape[0]
    strips = lax.axis_size("tile")
    groups = lax.axis_size("atom")
    atom_at = lax.axis_index("atom")
    member = atom_at // 2
    core = atom_at % 2
    chips = [[i for i in range(groups) if i % 2 == side] for side in range(2)]
    swap = [(i, i ^ 1) for i in range(groups)]
    half = groups // 2
    pairs = []
    for s in range(strips):
        for a in range(groups):
            if a < half:
                pairs.append((s * groups + a, (s + strips - 1) % strips * groups + a + half))
            else:
                pairs.append((s * groups + a, (s + 1) % strips * groups + a - half))

    def exchange(field):
        return lax.all_to_all(field, "atom", 0, 0, tiled=True, axis_index_groups=chips)

    params = pltpu.CompilerParams(vmem_limit_bytes=48 * 1024 * 1024)
    flops = 2 * 72 * atoms * C * TAP * TILE_W
    cost = pl.CostEstimate(flops=flops, bytes_accessed=3 << 20, transcendentals=0)
    a_corr, a_synth = pl.pallas_call(
        atoms_kernel,
        out_shape=(
            jax.ShapeDtypeStruct((TAP * atoms, TAP * C), jnp.bfloat16),
            jax.ShapeDtypeStruct((2, TAP * HALF, TAP * atoms), jnp.bfloat16),
        ),
        in_specs=[VMEM],
        out_specs=(VMEM,) * 2,
        scratch_shapes=[
            pltpu.VMEM((C * atoms, 128), jnp.float32),
            pltpu.VMEM((atoms * TAP_ROWS, 128), jnp.float32),
            pltpu.VMEM((TAP * atoms, TAP * C), jnp.float32),
        ],
        compiler_params=params,
        cost_estimate=cost,
    )(dictionary)
    sums = jax.ShapeDtypeStruct((ROWS, 2, HALF, TILE_W), jnp.float32)
    room = [
        pltpu.VMEM((2, TAP * atoms, TILE_W), jnp.bfloat16),
        pltpu.VMEM((2 * ROWS * HALF, TILE_W), jnp.float32),
    ]
    half_cost = pl.CostEstimate(flops=flops // 2, bytes_accessed=3 << 20, transcendentals=0)
    send, coef_rows, edges = pl.pallas_call(
        send_kernel,
        out_shape=(
            sums,
            jax.ShapeDtypeStruct((ROWS, atoms, TILE_W), jnp.bfloat16),
            jax.ShapeDtypeStruct((2, TILE_W), jnp.bfloat16),
        ),
        in_specs=[VMEM] * 3,
        out_specs=(VMEM,) * 3,
        scratch_shapes=room,
        compiler_params=params,
        cost_estimate=half_cost,
    )(coeffs, a_synth, seam_map)
    keep = pl.pallas_call(
        keep_kernel,
        out_shape=sums,
        in_specs=[VMEM] * 3,
        out_specs=VMEM,
        scratch_shapes=room,
        compiler_params=params,
        cost_estimate=half_cost,
    )(coef_rows, a_synth, edges)
    image_row = lax.dynamic_slice(image, (core * HALF, member, 0), (HALF, 1, TILE_W))[:, 0]
    other = lax.ppermute(send.astype(jnp.float16), "atom", swap)
    partial = (keep + other.astype(jnp.float32)).astype(jnp.float16)
    partial, image_row, threshold = lax.optimization_barrier((partial, image_row, shrink[:, None]))
    pieces = exchange(partial)
    total = jnp.sum(pieces.astype(jnp.float32), axis=0)
    held = jnp.stack([image_row.astype(jnp.float32) - total[0], total[1]])
    facing = lax.ppermute(held, ("tile", "atom"), pairs)
    rows_two = jnp.stack([held[0] - facing[1], facing[0] - held[1]]).astype(jnp.bfloat16)
    mine = exchange(jnp.broadcast_to(rows_two[None], (ROWS, 2, HALF, TILE_W)))
    theirs = lax.ppermute(mine, "atom", swap)

    scale = float((ROWS * strips * TILE_W) ** -0.5) * SHRINK_TERMS
    per = C // strips
    term_half = pl.pallas_call(
        functools.partial(terms_kernel, scale=scale),
        out_shape=jax.ShapeDtypeStruct((strips // 2, TAP * per, LANES), jnp.float32),
        in_specs=[VMEM] * 3,
        out_specs=VMEM,
        scratch_shapes=[
            pltpu.VMEM((2, TAP * HALF, ROWS * TILE_W), jnp.bfloat16),
            pltpu.VMEM((2, ROWS * atoms, ROWS * TILE_W), jnp.bfloat16),
        ],
        compiler_params=params,
        cost_estimate=half_cost,
    )
    my_terms = term_half(mine, edges, coef_rows)
    their_terms = term_half(theirs, edges, coef_rows)
    first = core == 0
    terms = jnp.concatenate(
        [jnp.where(first, my_terms, their_terms), jnp.where(first, their_terms, my_terms)]
    ).astype(jnp.float16)
    got = lax.all_to_all(terms, "tile", 0, 0, tiled=True)
    new_coeffs, residual = pl.pallas_call(
        coeffs_kernel,
        out_shape=(
            jax.ShapeDtypeStruct((atoms, ROWS, TILE_W), jnp.bfloat16),
            jax.ShapeDtypeStruct((C, ROWS, TILE_W), jnp.bfloat16),
        ),
        in_specs=[VMEM] * 6,
        out_specs=(VMEM,) * 2,
        scratch_shapes=[
            pltpu.VMEM((2, TAP * C, TILE_W), jnp.bfloat16),
            pltpu.VMEM((ROWS * atoms, TILE_W), jnp.float32),
            pltpu.VMEM((ROWS, C, TILE_W), jnp.bfloat16),
        ],
        compiler_params=params,
        cost_estimate=cost,
    )(mine, theirs, edges, coef_rows, a_corr, threshold)
    step = jnp.sum(got.astype(jnp.float32), axis=0)[:, : TAP * atoms] * (1.0 / SHRINK_TERMS)
    step = step.reshape(TAP, per, TAP, atoms)
    atom_step = step.transpose(3, 1, 2, 0).reshape(atoms, per * TAPS)
    return (new_coeffs, residual, atom_step)


def solution(mesh):
    placed = (P(None, "tile", None), P("atom", "tile", None), P("atom", None), P("atom"), P())
    return jax.shard_map(
        per_device,
        mesh=mesh,
        in_specs=placed,
        out_specs=(P("atom", "tile", None), P(None, "tile", None), P("atom", "tile")),
        check_vma=False,
    )
```

```python
import functools

import jax
import jax.numpy as jnp
from jax import lax
from jax.experimental import pallas as pl
from jax.experimental.pallas import tpu as pltpu
from jax.sharding import PartitionSpec as P

C = 64
TAP = 9
TAPS = TAP * TAP
TILE_W = 512
HALO = TAP // 2
LEFT = 128 - HALO
HALF = C // 2
ROWS = 8
TAP_ROWS = 88
LANES = 256
SHRINK_TERMS = 2.0**-6

step_size = 0.1
eps_sq = 0.01


def seam_weight(seam_ref, at):
    seam = seam_ref[pl.ds(at, 1), :].astype(jnp.float32)
    return (0.5 + 0.5 * seam).astype(jnp.bfloat16)


def turn(block):
    return jnp.swapaxes(block.astype(jnp.float32), 0, 1).astype(jnp.bfloat16)


def shifted(row, j):
    zero = jnp.zeros((row.shape[0], 128), row.dtype)
    wide = jnp.concatenate([zero, row, zero], axis=1)
    return wide[:, LEFT + j : LEFT + j + TILE_W]


def atoms_kernel(d_ref, acorr_ref, asynth_ref, by_band, by_atom, turned):
    atoms = d_ref.shape[0]
    d = d_ref[...].astype(jnp.float32)
    for c in range(C):
        by_band[c * atoms : (c + 1) * atoms, 0:TAPS] = d[:, c * TAPS : (c + 1) * TAPS]
    for k in range(atoms):
        block = by_band[pl.ds(k, C, stride=atoms), :]
        by_atom[k * TAP_ROWS : (k + 1) * TAP_ROWS, 0:C] = jnp.transpose(block)[0:TAP_ROWS, :]
    for tap in range(TAPS):
        dy, dx = divmod(tap, TAP)
        block = by_atom[pl.ds(tap, atoms, stride=TAP_ROWS), :][:, 0:C]
        acorr_ref[dy * atoms : (dy + 1) * atoms, dx * C : (dx + 1) * C] = block.astype(jnp.bfloat16)
        turned[dx * atoms : (dx + 1) * atoms, dy * C : (dy + 1) * C] = block
    bands = jnp.transpose(turned[...]).astype(jnp.bfloat16)
    for dy in range(TAP):
        for half in range(2):
            asynth_ref[half, dy * HALF : (dy + 1) * HALF, :] = bands[
                dy * C + half * HALF : dy * C + (half + 1) * HALF, :
            ]


def synthesize(a, rows_ref, w_up, w_down, out_ref, cols, acc):
    atoms = rows_ref.shape[1]
    acc[...] = jnp.zeros_like(acc)

    def add(slot, q, low, high):
        dy = low - (ROWS - 1) + q
        count = high - low + 1
        acc[low * HALF : (high + 1) * HALF, :] += jnp.dot(
            a[dy * HALF : (dy + count) * HALF, :], cols[slot], preferred_element_type=jnp.float32
        )

    for q in range(ROWS):
        row = rows_ref[q]
        weight = w_up if q < HALO else w_down
        for slot, field in ((0, row), (1, row * weight)):
            for dx in range(TAP):
                cols[slot, dx * atoms : (dx + 1) * atoms, :] = shifted(field, dx)
        low, high = ROWS - 1 - q, ROWS + TAP - 2 - q
        add(0, q, max(HALO, low), min(HALO + ROWS - 1, high))
        if q < HALO:
            add(1, q, HALO + ROWS, high)
        else:
            add(1, q, low, HALO - 1)
    for j in range(ROWS):
        edge = HALO + ROWS + (HALO - 1) - j if j < HALO else ROWS - 1 - j
        for part, at in ((0, HALO + ROWS - 1 - j), (1, edge)):
            out_ref[j, part] = acc[at * HALF : (at + 1) * HALF, :]


def send_kernel(coef_ref, a_ref, seam_ref, send_ref, rows_ref, edge_ref, cols, acc):
    position = lax.axis_index("tile")
    strips = seam_ref.shape[0]
    w_up = seam_weight(seam_ref, lax.rem(position + (strips - 1), strips))
    w_down = seam_weight(seam_ref, position)
    edge_ref[0:1, :] = w_up
    edge_ref[1:2, :] = w_down
    rows_ref[...] = turn(coef_ref[...])
    a = a_ref[1 - lax.rem(lax.axis_index("atom"), 2)]
    synthesize(a, rows_ref, w_up, w_down, send_ref, cols, acc)


def keep_kernel(rows_ref, a_ref, edge_ref, keep_ref, cols, acc):
    a = a_ref[lax.rem(lax.axis_index("atom"), 2)]
    synthesize(a, rows_ref, edge_ref[0:1, :], edge_ref[1:2, :], keep_ref, cols, acc)


def pad_row(core, mine_ref, other_ref, w_up, w_down, r):
    if r < HALO:
        at, part = r, 1
    elif r < HALO + ROWS:
        at, part = r - HALO, 0
    else:
        at, part = r - ROWS, 1
    mine, other = mine_ref[at, part], other_ref[at, part]
    first = core == 0
    row = jnp.concatenate(
        [jnp.where(first, mine, other), jnp.where(first, other, mine)], axis=0
    )
    if r < HALO:
        return row * w_up
    if r >= HALO + ROWS:
        return row * w_down
    return row


def met(r):
    first, last = max(0, r - (TAP - 1)), min(ROWS - 1, r)
    return first, last, first + TAP - 1 - r, last + TAP - 1 - r


def terms_kernel(half_ref, edge_ref, coef_ref, term_ref, cols, lags, scale):
    atoms = coef_ref.shape[1]
    wide = ROWS * TILE_W
    sums = []
    for part in range(2):
        for i in range(ROWS):
            r = part * ROWS + i
            if r < HALO:
                row = half_ref[r, 1] * edge_ref[0:1, :]
            elif r < HALO + ROWS:
                row = half_ref[r - HALO, 0]
            else:
                row = half_ref[r - ROWS, 1] * edge_ref[1:2, :]
            columns = slice(i * TILE_W, (i + 1) * TILE_W)
            for dx in range(TAP):
                cols[part, dx * HALF : (dx + 1) * HALF, columns] = shifted(row, TAP - 1 - dx)
            for at in range(ROWS):
                y = r - (ROWS - 1) - part + at
                there = 0 <= y < ROWS
                lags[part, at * atoms : (at + 1) * atoms, columns] = (
                    coef_ref[y] if there else jnp.zeros((atoms, TILE_W), jnp.bfloat16)
                )
        sums.append(
            lax.dot_general(
                cols[part], lags[part], (((1,), (1,)), ((), ())), preferred_element_type=jnp.float32
            )
        )
    edge = jnp.zeros((TAP * HALF, atoms), jnp.float32)
    total = jnp.concatenate([edge, sums[0]], axis=1) + jnp.concatenate([sums[1], edge], axis=1)
    total = total * scale
    parts = term_ref.shape[0]
    per = HALF // parts
    main = TAP * per
    for t in range(parts):
        blocks = [total[dx * HALF + t * per : dx * HALF + (t + 1) * per, :] for dx in range(TAP)]
        for dx in range(TAP):
            term_ref[t, dx * per : (dx + 1) * per, :] = blocks[dx][:, :LANES]
        rest = [block[:, LANES:] for block in blocks]
        term_ref[t, main : main + per, :] = jnp.concatenate(rest[:-1], axis=1)
        gap = jnp.zeros((per, LANES - atoms), jnp.float32)
        term_ref[t, main + per : main + 2 * per, :] = jnp.concatenate([rest[-1], gap], axis=1)


def coeffs_kernel(
    mine_ref, other_ref, edge_ref, coef_ref, a_ref, shrink_ref,
    new_ref, resid_ref, cols, acc, own,
):
    atoms = coef_ref.shape[1]
    core = lax.rem(lax.axis_index("atom"), 2)
    w_up, w_down = edge_ref[0:1, :], edge_ref[1:2, :]
    acc[...] = jnp.zeros_like(acc)
    for r in range(ROWS + TAP - 1):
        row = pad_row(core, mine_ref, other_ref, w_up, w_down, r)
        if HALO <= r < HALO + ROWS:
            own[r - HALO] = row
        slot = r % 2
        for dx in range(TAP):
            cols[slot, dx * C : (dx + 1) * C, :] = shifted(row, TAP - 1 - dx)
        first, last, low, high = met(r)
        acc[first * atoms : (last + 1) * atoms, :] += jnp.dot(
            a_ref[low * atoms : (high + 1) * atoms, :], cols[slot], preferred_element_type=jnp.float32
        )
    u = coef_ref[...].reshape(ROWS * atoms, TILE_W).astype(jnp.float32) + step_size * acc[...]
    threshold = jnp.concatenate([shrink_ref[:, 0:1]] * ROWS, axis=0)
    u = u - threshold * u / jnp.sqrt(u * u + eps_sq)
    new_ref[...] = turn(u.reshape(ROWS, atoms, TILE_W))
    resid_ref[...] = turn(own[...])


VMEM = pl.BlockSpec(memory_space=pltpu.VMEM)


def per_device(image, coeffs, dictionary, shrink, seam_map):
    atoms = coeffs.shape[0]
    strips = lax.axis_size("tile")
    groups = lax.axis_size("atom")
    atom_at = lax.axis_index("atom")
    member = atom_at // 2
    core = atom_at % 2
    chips = [[i for i in range(groups) if i % 2 == side] for side in range(2)]
    swap = [(i, i ^ 1) for i in range(groups)]
    half = groups // 2
    pairs = []
    for s in range(strips):
        for a in range(groups):
            if a < half:
                pairs.append((s * groups + a, (s + strips - 1) % strips * groups + a + half))
            else:
                pairs.append((s * groups + a, (s + 1) % strips * groups + a - half))

    def exchange(field):
        return lax.all_to_all(field, "atom", 0, 0, tiled=True, axis_index_groups=chips)

    params = pltpu.CompilerParams(vmem_limit_bytes=48 * 1024 * 1024)
    flops = 2 * 72 * atoms * C * TAP * TILE_W
    cost = pl.CostEstimate(flops=flops, bytes_accessed=3 << 20, transcendentals=0)
    a_corr, a_synth = pl.pallas_call(
        atoms_kernel,
        out_shape=(
            jax.ShapeDtypeStruct((TAP * atoms, TAP * C), jnp.bfloat16),
            jax.ShapeDtypeStruct((2, TAP * HALF, TAP * atoms), jnp.bfloat16),
        ),
        in_specs=[VMEM],
        out_specs=(VMEM,) * 2,
        scratch_shapes=[
            pltpu.VMEM((C * atoms, 128), jnp.float32),
            pltpu.VMEM((atoms * TAP_ROWS, 128), jnp.float32),
            pltpu.VMEM((TAP * atoms, TAP * C), jnp.float32),
        ],
        compiler_params=params,
        cost_estimate=cost,
    )(dictionary)
    sums = jax.ShapeDtypeStruct((ROWS, 2, HALF, TILE_W), jnp.float32)
    room = [
        pltpu.VMEM((2, TAP * atoms, TILE_W), jnp.bfloat16),
        pltpu.VMEM((2 * ROWS * HALF, TILE_W), jnp.float32),
    ]
    half_cost = pl.CostEstimate(flops=flops // 2, bytes_accessed=3 << 20, transcendentals=0)
    send, coef_rows, edges = pl.pallas_call(
        send_kernel,
        out_shape=(
            sums,
            jax.ShapeDtypeStruct((ROWS, atoms, TILE_W), jnp.bfloat16),
            jax.ShapeDtypeStruct((2, TILE_W), jnp.bfloat16),
        ),
        in_specs=[VMEM] * 3,
        out_specs=(VMEM,) * 3,
        scratch_shapes=room,
        compiler_params=params,
        cost_estimate=half_cost,
    )(coeffs, a_synth, seam_map)
    keep = pl.pallas_call(
        keep_kernel,
        out_shape=sums,
        in_specs=[VMEM] * 3,
        out_specs=VMEM,
        scratch_shapes=room,
        compiler_params=params,
        cost_estimate=half_cost,
    )(coef_rows, a_synth, edges)
    image_row = lax.dynamic_slice(image, (core * HALF, member, 0), (HALF, 1, TILE_W))[:, 0]
    other = lax.ppermute(send.astype(jnp.float16), "atom", swap)
    partial = (keep + other.astype(jnp.float32)).astype(jnp.float16)
    partial, image_row = lax.optimization_barrier((partial, image_row))
    pieces = exchange(partial)
    total = jnp.sum(pieces.astype(jnp.float32), axis=0)
    held = jnp.stack([image_row.astype(jnp.float32) - total[0], total[1]])
    held, shrink = lax.optimization_barrier((held, shrink))
    facing = lax.ppermute(held, ("tile", "atom"), pairs)
    threshold = jnp.broadcast_to(shrink[:, None], (atoms, 128))
    facing, threshold = lax.optimization_barrier((facing, threshold))
    rows_two = jnp.stack([held[0] - facing[1], facing[0] - held[1]]).astype(jnp.bfloat16)
    mine = exchange(jnp.broadcast_to(rows_two[None], (ROWS, 2, HALF, TILE_W)))
    theirs = lax.ppermute(mine, "atom", swap)

    scale = float((ROWS * strips * TILE_W) ** -0.5) * SHRINK_TERMS
    per = C // strips
    term_half = pl.pallas_call(
        functools.partial(terms_kernel, scale=scale),
        out_shape=jax.ShapeDtypeStruct((strips // 2, (TAP + 2) * per, LANES), jnp.float32),
        in_specs=[VMEM] * 3,
        out_specs=VMEM,
        scratch_shapes=[
            pltpu.VMEM((2, TAP * HALF, ROWS * TILE_W), jnp.bfloat16),
            pltpu.VMEM((2, ROWS * atoms, ROWS * TILE_W), jnp.bfloat16),
        ],
        compiler_params=params,
        cost_estimate=half_cost,
    )
    my_terms = term_half(mine, edges, coef_rows)
    their_terms = term_half(theirs, edges, coef_rows)
    first = core == 0
    side = lax.axis_index("tile") % 2 == 0
    terms = jnp.concatenate(
        [jnp.where(first, my_terms, their_terms), jnp.where(first, their_terms, my_terms)]
    ).reshape(strips // 2, 2, (TAP + 2) * per, LANES)
    away = jnp.where(side, terms[:, 1], terms[:, 0]).astype(jnp.float16)
    stay = jnp.where(side, terms[:, 0], terms[:, 1])
    across = lax.ppermute(away, "tile", [(i, i ^ 1) for i in range(strips)])
    new_coeffs, residual = pl.pallas_call(
        coeffs_kernel,
        out_shape=(
            jax.ShapeDtypeStruct((atoms, ROWS, TILE_W), jnp.bfloat16),
            jax.ShapeDtypeStruct((C, ROWS, TILE_W), jnp.bfloat16),
        ),
        in_specs=[VMEM] * 6,
        out_specs=(VMEM,) * 2,
        scratch_shapes=[
            pltpu.VMEM((2, TAP * C, TILE_W), jnp.bfloat16),
            pltpu.VMEM((ROWS * atoms, TILE_W), jnp.float32),
            pltpu.VMEM((ROWS, C, TILE_W), jnp.bfloat16),
        ],
        compiler_params=params,
        cost_estimate=cost,
    )(mine, theirs, edges, coef_rows, a_corr, threshold)
    across, new_coeffs, residual = lax.optimization_barrier((across, new_coeffs, residual))
    pair_terms = (stay + across.astype(jnp.float32)).astype(jnp.float16)
    lines = strips // 2
    line = lax.axis_index("tile") // 2
    ahead = lax.dynamic_slice(
        jnp.concatenate([pair_terms, pair_terms]), (line, 0, 0), (lines, (TAP + 2) * per, LANES)
    )
    got = [ahead[0]]
    for hops in (2, 1, 3):
        route = [(i, (i + 2 * hops) % strips) for i in range(strips)]
        got.append(lax.ppermute(ahead[hops], "tile", route))
    step = sum(piece.astype(jnp.float32) for piece in got) * (1.0 / SHRINK_TERMS)
    main = step[: TAP * per].reshape(TAP, per, TAP - 1, atoms)
    rest = step[TAP * per : (TAP + 1) * per].reshape(per, TAP - 1, atoms).transpose(1, 0, 2)
    rest = jnp.concatenate([rest, step[None, (TAP + 1) * per :, :atoms]])
    step = jnp.concatenate([main, rest[:, :, None, :]], axis=2)
    atom_step = step.transpose(3, 1, 2, 0).reshape(atoms, per * TAPS)
    return (new_coeffs, residual, atom_step)


def solution(mesh):
    placed = (P(None, "tile", None), P("atom", "tile", None), P("atom", None), P("atom"), P())
    return jax.shard_map(
        per_device,
        mesh=mesh,
        in_specs=placed,
        out_specs=(P("atom", "tile", None), P(None, "tile", None), P("atom", "tile")),
        check_vma=False,
    )
```

```python
import functools

import jax
import jax.numpy as jnp
from jax import lax
from jax.experimental import pallas as pl
from jax.experimental.pallas import tpu as pltpu
from jax.sharding import PartitionSpec as P

C = 64
TAP = 9
TAPS = TAP * TAP
TILE_W = 512
HALO = TAP // 2
LEFT = 128 - HALO
HALF = C // 2
ROWS = 8
TAP_ROWS = 88
LANES = 256
SHRINK_TERMS = 2.0**-6

step_size = 0.1
eps_sq = 0.01


def seam_weight(seam_ref, at):
    seam = seam_ref[pl.ds(at, 1), :].astype(jnp.float32)
    return (0.5 + 0.5 * seam).astype(jnp.bfloat16)


def turn(block):
    return jnp.swapaxes(block.astype(jnp.float32), 0, 1).astype(jnp.bfloat16)


def shifted(row, j):
    zero = jnp.zeros((row.shape[0], 128), row.dtype)
    wide = jnp.concatenate([zero, row, zero], axis=1)
    return wide[:, LEFT + j : LEFT + j + TILE_W]


def atoms_kernel(d_ref, acorr_ref, asynth_ref, by_band, by_atom, turned):
    atoms = d_ref.shape[0]
    d = d_ref[...].astype(jnp.float32)
    for c in range(C):
        by_band[c * atoms : (c + 1) * atoms, 0:TAPS] = d[:, c * TAPS : (c + 1) * TAPS]
    for k in range(atoms):
        block = by_band[pl.ds(k, C, stride=atoms), :]
        by_atom[k * TAP_ROWS : (k + 1) * TAP_ROWS, 0:C] = jnp.transpose(block)[0:TAP_ROWS, :]
    for tap in range(TAPS):
        dy, dx = divmod(tap, TAP)
        block = by_atom[pl.ds(tap, atoms, stride=TAP_ROWS), :][:, 0:C]
        acorr_ref[dy * atoms : (dy + 1) * atoms, dx * C : (dx + 1) * C] = block.astype(jnp.bfloat16)
        turned[dx * atoms : (dx + 1) * atoms, dy * C : (dy + 1) * C] = block
    bands = jnp.transpose(turned[...]).astype(jnp.bfloat16)
    for dy in range(TAP):
        for half in range(2):
            asynth_ref[half, dy * HALF : (dy + 1) * HALF, :] = bands[
                dy * C + half * HALF : dy * C + (half + 1) * HALF, :
            ]


def synthesize(a, rows_ref, w_up, w_down, out_ref, cols, acc):
    atoms = rows_ref.shape[1]
    acc[...] = jnp.zeros_like(acc)

    def add(slot, q, low, high):
        dy = low - (ROWS - 1) + q
        count = high - low + 1
        acc[low * HALF : (high + 1) * HALF, :] += jnp.dot(
            a[dy * HALF : (dy + count) * HALF, :], cols[slot], preferred_element_type=jnp.float32
        )

    for q in range(ROWS):
        row = rows_ref[q]
        weight = w_up if q < HALO else w_down
        for slot, field in ((0, row), (1, row * weight)):
            for dx in range(TAP):
                cols[slot, dx * atoms : (dx + 1) * atoms, :] = shifted(field, dx)
        low, high = ROWS - 1 - q, ROWS + TAP - 2 - q
        add(0, q, max(HALO, low), min(HALO + ROWS - 1, high))
        if q < HALO:
            add(1, q, HALO + ROWS, high)
        else:
            add(1, q, low, HALO - 1)
    for j in range(ROWS):
        edge = HALO + ROWS + (HALO - 1) - j if j < HALO else ROWS - 1 - j
        for part, at in ((0, HALO + ROWS - 1 - j), (1, edge)):
            out_ref[j, part] = acc[at * HALF : (at + 1) * HALF, :]


def send_kernel(coef_ref, a_ref, seam_ref, send_ref, rows_ref, edge_ref, cols, acc):
    position = lax.axis_index("tile")
    strips = seam_ref.shape[0]
    w_up = seam_weight(seam_ref, lax.rem(position + (strips - 1), strips))
    w_down = seam_weight(seam_ref, position)
    edge_ref[0:1, :] = w_up
    edge_ref[1:2, :] = w_down
    rows_ref[...] = turn(coef_ref[...])
    a = a_ref[1 - lax.rem(lax.axis_index("atom"), 2)]
    synthesize(a, rows_ref, w_up, w_down, send_ref, cols, acc)


def keep_kernel(rows_ref, a_ref, edge_ref, keep_ref, cols, acc):
    a = a_ref[lax.rem(lax.axis_index("atom"), 2)]
    synthesize(a, rows_ref, edge_ref[0:1, :], edge_ref[1:2, :], keep_ref, cols, acc)


def pad_row(core, mine_ref, other_ref, w_up, w_down, r):
    if r < HALO:
        at, part = r, 1
    elif r < HALO + ROWS:
        at, part = r - HALO, 0
    else:
        at, part = r - ROWS, 1
    mine, other = mine_ref[at, part], other_ref[at, part]
    first = core == 0
    row = jnp.concatenate(
        [jnp.where(first, mine, other), jnp.where(first, other, mine)], axis=0
    )
    if r < HALO:
        return row * w_up
    if r >= HALO + ROWS:
        return row * w_down
    return row


def met(r):
    first, last = max(0, r - (TAP - 1)), min(ROWS - 1, r)
    return first, last, first + TAP - 1 - r, last + TAP - 1 - r


def terms_kernel(half_ref, edge_ref, coef_ref, term_ref, cols, lags, scale):
    atoms = coef_ref.shape[1]
    wide = ROWS * TILE_W
    sums = []
    for part in range(2):
        for i in range(ROWS):
            r = part * ROWS + i
            if r < HALO:
                row = half_ref[r, 1] * edge_ref[0:1, :]
            elif r < HALO + ROWS:
                row = half_ref[r - HALO, 0]
            else:
                row = half_ref[r - ROWS, 1] * edge_ref[1:2, :]
            columns = slice(i * TILE_W, (i + 1) * TILE_W)
            for dx in range(TAP):
                cols[part, dx * HALF : (dx + 1) * HALF, columns] = shifted(row, TAP - 1 - dx)
            for at in range(ROWS):
                y = r - (ROWS - 1) - part + at
                there = 0 <= y < ROWS
                lags[part, at * atoms : (at + 1) * atoms, columns] = (
                    coef_ref[y] if there else jnp.zeros((atoms, TILE_W), jnp.bfloat16)
                )
        sums.append(
            lax.dot_general(
                cols[part], lags[part], (((1,), (1,)), ((), ())), preferred_element_type=jnp.float32
            )
        )
    edge = jnp.zeros((TAP * HALF, atoms), jnp.float32)
    total = jnp.concatenate([edge, sums[0]], axis=1) + jnp.concatenate([sums[1], edge], axis=1)
    total = total * scale
    parts = term_ref.shape[0]
    per = HALF // parts
    main = TAP * per
    for t in range(parts):
        blocks = [total[dx * HALF + t * per : dx * HALF + (t + 1) * per, :] for dx in range(TAP)]
        for dx in range(TAP):
            term_ref[t, dx * per : (dx + 1) * per, :] = blocks[dx][:, :LANES]
        rest = [block[:, LANES:] for block in blocks]
        term_ref[t, main : main + per, :] = jnp.concatenate(rest[:-1], axis=1)
        gap = jnp.zeros((per, LANES - atoms), jnp.float32)
        term_ref[t, main + per : main + 2 * per, :] = jnp.concatenate([rest[-1], gap], axis=1)


def coeffs_kernel(
    mine_ref, other_ref, edge_ref, coef_ref, a_ref, shrink_ref,
    new_ref, resid_ref, cols, acc, own,
):
    atoms = coef_ref.shape[1]
    core = lax.rem(lax.axis_index("atom"), 2)
    w_up, w_down = edge_ref[0:1, :], edge_ref[1:2, :]
    acc[...] = jnp.zeros_like(acc)
    for r in range(ROWS + TAP - 1):
        row = pad_row(core, mine_ref, other_ref, w_up, w_down, r)
        if HALO <= r < HALO + ROWS:
            own[r - HALO] = row
        slot = r % 2
        for dx in range(TAP):
            cols[slot, dx * C : (dx + 1) * C, :] = shifted(row, TAP - 1 - dx)
        first, last, low, high = met(r)
        acc[first * atoms : (last + 1) * atoms, :] += jnp.dot(
            a_ref[low * atoms : (high + 1) * atoms, :], cols[slot], preferred_element_type=jnp.float32
        )
    u = coef_ref[...].reshape(ROWS * atoms, TILE_W).astype(jnp.float32) + step_size * acc[...]
    threshold = jnp.concatenate([shrink_ref[:, 0:1]] * ROWS, axis=0)
    u = u - threshold * u / jnp.sqrt(u * u + eps_sq)
    new_ref[...] = turn(u.reshape(ROWS, atoms, TILE_W))
    resid_ref[...] = turn(own[...])


VMEM = pl.BlockSpec(memory_space=pltpu.VMEM)


def per_device(image, coeffs, dictionary, shrink, seam_map):
    atoms = coeffs.shape[0]
    strips = lax.axis_size("tile")
    groups = lax.axis_size("atom")
    atom_at = lax.axis_index("atom")
    member = atom_at // 2
    core = atom_at % 2
    chips = [[i for i in range(groups) if i % 2 == side] for side in range(2)]
    swap = [(i, i ^ 1) for i in range(groups)]
    half = groups // 2
    pairs = []
    for s in range(strips):
        for a in range(groups):
            if a < half:
                pairs.append((s * groups + a, (s + strips - 1) % strips * groups + a + half))
            else:
                pairs.append((s * groups + a, (s + 1) % strips * groups + a - half))

    def exchange(field):
        return lax.all_to_all(field, "atom", 0, 0, tiled=True, axis_index_groups=chips)

    params = pltpu.CompilerParams(vmem_limit_bytes=48 * 1024 * 1024)
    flops = 2 * 72 * atoms * C * TAP * TILE_W
    cost = pl.CostEstimate(flops=flops, bytes_accessed=3 << 20, transcendentals=0)
    a_corr, a_synth = pl.pallas_call(
        atoms_kernel,
        out_shape=(
            jax.ShapeDtypeStruct((TAP * atoms, TAP * C), jnp.bfloat16),
            jax.ShapeDtypeStruct((2, TAP * HALF, TAP * atoms), jnp.bfloat16),
        ),
        in_specs=[VMEM],
        out_specs=(VMEM,) * 2,
        scratch_shapes=[
            pltpu.VMEM((C * atoms, 128), jnp.float32),
            pltpu.VMEM((atoms * TAP_ROWS, 128), jnp.float32),
            pltpu.VMEM((TAP * atoms, TAP * C), jnp.float32),
        ],
        compiler_params=params,
        cost_estimate=cost,
    )(dictionary)
    sums = jax.ShapeDtypeStruct((ROWS, 2, HALF, TILE_W), jnp.float32)
    room = [
        pltpu.VMEM((2, TAP * atoms, TILE_W), jnp.bfloat16),
        pltpu.VMEM((2 * ROWS * HALF, TILE_W), jnp.float32),
    ]
    half_cost = pl.CostEstimate(flops=flops // 2, bytes_accessed=3 << 20, transcendentals=0)
    send, coef_rows, edges = pl.pallas_call(
        send_kernel,
        out_shape=(
            sums,
            jax.ShapeDtypeStruct((ROWS, atoms, TILE_W), jnp.bfloat16),
            jax.ShapeDtypeStruct((2, TILE_W), jnp.bfloat16),
        ),
        in_specs=[VMEM] * 3,
        out_specs=(VMEM,) * 3,
        scratch_shapes=room,
        compiler_params=params,
        cost_estimate=half_cost,
    )(coeffs, a_synth, seam_map)
    keep = pl.pallas_call(
        keep_kernel,
        out_shape=sums,
        in_specs=[VMEM] * 3,
        out_specs=VMEM,
        scratch_shapes=room,
        compiler_params=params,
        cost_estimate=half_cost,
    )(coef_rows, a_synth, edges)
    image_row = lax.dynamic_slice(image, (core * HALF, member, 0), (HALF, 1, TILE_W))[:, 0]
    other = lax.ppermute(send.astype(jnp.float16), "atom", swap)
    partial = (keep + other.astype(jnp.float32)).astype(jnp.float16)
    partial, image_row = lax.optimization_barrier((partial, image_row))
    pieces = exchange(partial)
    total = jnp.sum(pieces.astype(jnp.float32), axis=0)
    held = jnp.stack([image_row.astype(jnp.float32) - total[0], total[1]])
    held, shrink = lax.optimization_barrier((held.astype(jnp.float16), shrink))
    facing = lax.ppermute(held, ("tile", "atom"), pairs)
    threshold = jnp.broadcast_to(shrink[:, None], (atoms, 128))
    facing, threshold = lax.optimization_barrier((facing, threshold))
    held, facing = held.astype(jnp.float32), facing.astype(jnp.float32)
    rows_two = jnp.stack([held[0] - facing[1], facing[0] - held[1]]).astype(jnp.bfloat16)
    mine = exchange(jnp.broadcast_to(rows_two[None], (ROWS, 2, HALF, TILE_W)))
    theirs = lax.ppermute(mine, "atom", swap)

    scale = float((ROWS * strips * TILE_W) ** -0.5) * SHRINK_TERMS
    per = C // strips
    term_half = pl.pallas_call(
        functools.partial(terms_kernel, scale=scale),
        out_shape=jax.ShapeDtypeStruct((strips // 2, (TAP + 2) * per, LANES), jnp.float32),
        in_specs=[VMEM] * 3,
        out_specs=VMEM,
        scratch_shapes=[
            pltpu.VMEM((2, TAP * HALF, ROWS * TILE_W), jnp.bfloat16),
            pltpu.VMEM((2, ROWS * atoms, ROWS * TILE_W), jnp.bfloat16),
        ],
        compiler_params=params,
        cost_estimate=half_cost,
    )
    my_terms = term_half(mine, edges, coef_rows)
    their_terms = term_half(theirs, edges, coef_rows)
    first = core == 0
    side = lax.axis_index("tile") % 2 == 0
    terms = jnp.concatenate(
        [jnp.where(first, my_terms, their_terms), jnp.where(first, their_terms, my_terms)]
    ).reshape(strips // 2, 2, (TAP + 2) * per, LANES)
    away = jnp.where(side, terms[:, 1], terms[:, 0]).astype(jnp.float16)
    stay = jnp.where(side, terms[:, 0], terms[:, 1])
    across = lax.ppermute(away, "tile", [(i, i ^ 1) for i in range(strips)])
    new_coeffs, residual = pl.pallas_call(
        coeffs_kernel,
        out_shape=(
            jax.ShapeDtypeStruct((atoms, ROWS, TILE_W), jnp.bfloat16),
            jax.ShapeDtypeStruct((C, ROWS, TILE_W), jnp.bfloat16),
        ),
        in_specs=[VMEM] * 6,
        out_specs=(VMEM,) * 2,
        scratch_shapes=[
            pltpu.VMEM((2, TAP * C, TILE_W), jnp.bfloat16),
            pltpu.VMEM((ROWS * atoms, TILE_W), jnp.float32),
            pltpu.VMEM((ROWS, C, TILE_W), jnp.bfloat16),
        ],
        compiler_params=params,
        cost_estimate=cost,
    )(mine, theirs, edges, coef_rows, a_corr, threshold)
    across, new_coeffs, residual = lax.optimization_barrier((across, new_coeffs, residual))
    pair_terms = (stay + across.astype(jnp.float32)).astype(jnp.float16)
    lines = strips // 2
    line = lax.axis_index("tile") // 2
    ahead = lax.dynamic_slice(
        jnp.concatenate([pair_terms, pair_terms]), (line, 0, 0), (lines, (TAP + 2) * per, LANES)
    )
    got = [ahead[0]]
    for hops in (2, 1, 3):
        route = [(i, (i + 2 * hops) % strips) for i in range(strips)]
        got.append(lax.ppermute(ahead[hops], "tile", route))
    step = sum(piece.astype(jnp.float32) for piece in got) * (1.0 / SHRINK_TERMS)
    main = step[: TAP * per].reshape(TAP, per, TAP - 1, atoms)
    rest = step[TAP * per : (TAP + 1) * per].reshape(per, TAP - 1, atoms).transpose(1, 0, 2)
    rest = jnp.concatenate([rest, step[None, (TAP + 1) * per :, :atoms]])
    step = jnp.concatenate([main, rest[:, :, None, :]], axis=2)
    atom_step = step.transpose(3, 1, 2, 0).reshape(atoms, per * TAPS)
    return (new_coeffs, residual, atom_step)


def solution(mesh):
    placed = (P(None, "tile", None), P("atom", "tile", None), P("atom", None), P("atom"), P())
    return jax.shard_map(
        per_device,
        mesh=mesh,
        in_specs=placed,
        out_specs=(P("atom", "tile", None), P(None, "tile", None), P("atom", "tile")),
        check_vma=False,
    )
```
